512 devices in a mesh: dp: 32 (over x, y), row: 4 (over z_hi, core), col: 4 (over z_lo).
Axes of the slice: x: 4, y: 8, z: 8 (z_hi: 2, z_lo: 4; z = z_hi * 4 + z_lo), core: 2. Of those that a mesh axis runs over, the one named last changes fastest.
Arguments:
- grad_out: bfloat16 [32768, 8192], P('dp', ('col', 'row')), may hold values from -6 to 6
- weight: bfloat16 [28672, 8192], P(('dp', 'row'), 'col'), may hold values from -6 to 6
Outputs:
- gram: float32 [1024, 8192], P(('dp', 'row'), 'col')
- product: float32 [28672, 1024], P(('dp', 'row'), 'col')
The draws below stay inside these ranges and needn't reach their ends.
All inputs are finite; a program needn't handle non-finite values.
Results may differ from the reference program's by a relative error of at most 0.0029.
Values may be sent and summed in bfloat16 or wider, within the bound.
A program may use at most 64 MiB of HBM per device.

```python
import jax
import jax.numpy as jnp
from jax import lax

D = 8192
WIN_BLK = 64
TOK_DP = 1024
TOKENS = 32768
COLS = 28672
WROWS = 1024
N_DP = 32
N_ROW = 4
N_COL = 4


def with_spikes(array, stream_key, source, target, blocks, factor):
    owner, partner = [(jnp.arange(array.shape[position]) // (array.shape[position] // blocks)).reshape([-1 if axis == position else 1 for axis in range(array.ndim)]) for position in (source, target)]
    chosen = jax.random.permutation(stream_key, blocks)[partner]
    strong = (owner == chosen) | (owner == (partner + blocks // 2) % blocks)
    return jnp.where(strong, factor * array, array)


def levels(stream_key, extent, cuts, smallest, top_value):
    def one(dim, shards_of):
        draws = jax.random.uniform(jax.random.fold_in(jax.random.fold_in(stream_key, 6), dim), (shards_of,), jnp.float32, smallest / len(cuts), top_value / len(cuts))
        return jnp.repeat(jnp.exp(draws), extent[dim] // shards_of).reshape((-1,) + (1,) * (len(extent) - dim - 1))

    level = one(*cuts[0])
    for cut in cuts[1:]:
        level = level * one(*cut)
    return level


def centred(own_key, extent, scale, limit, shards=(), kind=jnp.bfloat16):
    entries = scale * jax.random.normal(own_key, extent, jnp.float32)
    if shards:
        entries = entries * levels(own_key, extent, shards, -0.22, 0.18)
    return jnp.clip(entries, -limit, limit).astype(kind)


def gaussian_with(rng, extent, width, bound, cuts, heavy, kind=jnp.bfloat16):
    entries = width * jax.random.normal(rng, extent, jnp.float32)
    if cuts:
        entries = entries * levels(rng, extent, cuts, -0.22, 0.18)
    return jnp.clip(with_spikes(entries, jax.random.fold_in(rng, 3), *heavy), -bound, bound).astype(kind)


def setup_inputs(seed: int = 0) -> dict:
    key_of = jax.random.split(jax.random.key(seed), 3)
    grad_out = gaussian_with(key_of[0], (TOKENS, D), 1.0, 6.0, ((0, 32), (1, 16)), (0, 1, 32, 2.75))
    weight = centred(key_of[1], (COLS, D), 1.0, 6.0, ((0, 128), (1, 4)))
    return dict(grad_out=grad_out, weight=weight)


def reference(grad_out, weight):
    total = grad_out.shape[0]
    block = D // (N_ROW * N_COL)
    per_dev = N_COL * WIN_BLK // N_DP
    parts = grad_out.reshape(total, N_COL, N_ROW, block)[:, :, :, :WIN_BLK]
    parts = jnp.transpose(parts, (0, 2, 1, 3)).reshape(total, N_ROW, N_DP, per_dev)
    window = jnp.transpose(parts, (0, 2, 1, 3)).reshape(total, WROWS)
    window_blocks = window.reshape(N_DP, TOK_DP, WROWS)
    grad_blocks = grad_out.reshape(N_DP, TOK_DP, D)

    def add_block(carry, pieces):
        left, right = pieces
        return carry + jnp.dot(left.T, right, preferred_element_type=jnp.float32), None

    gram_sum, unused = lax.scan(add_block, jnp.zeros((WROWS, D), jnp.float32), (window_blocks, grad_blocks))
    gram = gram_sum / TOKENS
    gram_low = gram.astype(jnp.bfloat16)
    product = lax.dot_general(weight, gram_low, (((1,), (1,)), ((), ())), preferred_element_type=jnp.float32)
    return gram, product
```

```python
import functools

import jax
import jax.numpy as jnp
from jax import lax
from jax.experimental import pallas as pl
from jax.experimental.pallas import tpu as pltpu
from jax.sharding import PartitionSpec as P

MESH = pl.DeviceIdType.MESH
F32, BF16 = jnp.float32, jnp.bfloat16
TOTAL = 32768
X_TYPE, Y_TYPE, Z_TYPE = BF16, F32, F32


def kernel(
    g_hbm, w_hbm, gram_ref, prod_ref,
    g, wt, part, own, x_in, s, y_in, t, gram_in, low, w, gl, q, z_in,
    load_sem, ring_send, ring_recv, sib_send, sib_recv, w_send, w_recv,
    x_send, x_recv, y_send, y_recv, h_send, h_recv, low_send, low_recv,
    ay_send, ay_recv, ax_send, ax_recv, z_send, z_recv,
):
    dp, row, c = lax.axis_index("dp"), lax.axis_index("row"), lax.axis_index("col")
    x, y, h, k = dp // 8, dp % 8, row // 2, row % 2
    z = h * 4 + c
    mate = 1 - k

    def at(px, py, pz, pk):
        return (px * 8 + py, (pz // 4) * 2 + pk, pz % 4)

    def copy(src, dst, send, recv, device):
        return pltpu.make_async_remote_copy(
            src_ref=src, dst_ref=dst, send_sem=send, recv_sem=recv,
            device_id=device, device_id_type=MESH,
        )

    sibling = at(x, y, z, mate)

    def arrived(dst, recv):
        copy(dst, dst, recv, recv, sibling).wait_recv()

    def sent(src, send):
        copy(src, src, send, send, sibling).wait_send()

    load_g = pltpu.make_async_copy(g_hbm, g, load_sem.at[0])
    load_w = pltpu.make_async_copy(w_hbm, w.at[k], load_sem.at[1])
    load_g.start()
    load_w.start()

    barrier = pltpu.get_barrier_semaphore()
    partners = [sibling]
    partners += [at((x + i) % 4, y, z, k) for i in range(1, 4)]
    for pk in range(2):
        partners += [at(x, (y + i) % 8, z, pk) for i in range(1, 8)]
        partners += [at(x, y, (z + i) % 8, pk) for i in range(1, 8)]
    for partner in partners:
        pl.semaphore_signal(barrier, inc=1, device_id=partner, device_id_type=MESH)

    def slot(pz, pk):
        return (pz % 4) * 4 + (pz // 4) * 2 + pk

    def half(b, j):
        return wt.at[b, pl.ds(32 * j, 32)]

    load_g.wait()
    mine = slot(z, k)
    wt[mine] = g[:, :128].astype(F32).T[:64].astype(BF16)
    load_w.wait()
    pl.semaphore_wait(barrier, len(partners))

    up, down = at(x, y, (z + 1) % 8, k), at(x, y, (z + 7) % 8, k)
    to = (up, down)

    def ring(direction, b, step, j):
        return copy(
            half(b, j), half(b, j), ring_send.at[direction, step, j],
            ring_recv.at[direction, step, j], to[direction],
        )

    def share(b, step, j):
        return copy(half(b, j), half(b, j), sib_send.at[step, j], sib_recv.at[step, j], sibling)

    for j in range(2):
        ring(0, mine, 0, j).start()
        ring(1, mine, 0, j).start()
    for j in range(2):
        share(mine, 0, j).start()
    w_copy = copy(w.at[k], w.at[k], w_send, w_recv, sibling)
    w_copy.start()
    for step in range(1, 4):
        for j in range(2):
            for direction in range(2):
                away = step if direction == 1 else 8 - step
                b = slot((z + away) % 8, k)
                arrived(half(b, j), ring_recv.at[direction, step - 1, j])
                if step < 3 or direction == j:
                    ring(direction, b, step, j).start()
                share(b, away, j).start()
    far = slot((z + 4) % 8, k)
    for j in range(2):
        arrived(half(far, j), ring_recv.at[j, 3, j])
        share(far, 4, j).start()
    for step in range(8):
        for j in range(2):
            arrived(half(slot((z + step) % 8, mate), j), sib_recv.at[step, j])

    def rows_of(px):
        left = wt[pl.ds(px * 4, 4)].reshape(256, 1024)
        got = jnp.dot(left, g[...], preferred_element_type=F32)
        return jnp.concatenate(
            [got[64 * r + 8 * i : 64 * r + 8 * i + 8] for i in range(8) for r in range(4)], axis=0
        )

    for n, away in enumerate((2, 1, 3)):
        px = (x + away) % 4
        part[n] = rows_of(px).astype(X_TYPE)
        copy(part.at[n], x_in.at[away - 1], x_send.at[away - 1], x_recv.at[away - 1], at(px, y, z, k)).start()
    own[...] = rows_of(x)
    for away in (1, 3, 2):
        arrived(x_in.at[away - 1], x_recv.at[away - 1])
    for i in range(8):
        rows = pl.ds(32 * i, 32)
        s[i] = own[rows] + x_in[0, rows].astype(F32) + x_in[1, rows].astype(F32) + x_in[2, rows].astype(F32)

    for away in (4, 3, 5, 2, 6, 1, 7):
        py = (y + away) % 8
        copy(s.at[py], y_in.at[away - 1], y_send.at[away - 1], y_recv.at[away - 1], at(x, py, z, k)).start()
    total = s[y]
    for away in (1, 7, 2, 6, 3, 5, 4):
        arrived(y_in.at[away - 1], y_recv.at[away - 1])
        total += y_in[away - 1]
    total = total * (1.0 / TOTAL)

    low[h] = total.astype(BF16)
    t[...] = total
    partner_low = copy(low.at[h], low.at[h], low_send, low_recv, at(x, y, (z + 4) % 8, k))
    partner_low.start()
    for away in range(1, 4):
        pr = (row + away) % 4
        copy(
            t.at[pl.ds(pl.multiple_of(8 * pr, 8), 8)], gram_in.at[row],
            h_send.at[away - 1], h_recv.at[away - 1], (dp, pr, c),
        ).start()
    gram_in[row] = t[pl.ds(pl.multiple_of(8 * row, 8), 8)]

    keeper = x // 2
    xi = x % 2

    def spread(ph, n):
        for away in (4, 3, 5, 2, 6, 1, 7):
            copy(
                low.at[ph], gl.at[xi, 2 * ph + k, y], ay_send.at[n, away],
                ay_recv.at[ph, k, away], at(x, (y + away) % 8, z, keeper),
            ).start()

        @pl.when(k == keeper)
        def _():
            gl[xi, 2 * ph + k, y] = low[ph]

        @pl.when(k != keeper)
        def _():
            copy(
                low.at[ph], gl.at[xi, 2 * ph + k, y], ay_send.at[n, 0], ay_recv.at[ph, k, 0], sibling
            ).start()

    spread(h, 0)
    arrived(low.at[1 - h], low_recv)
    spread(1 - h, 1)

    right, left = at((x + 1) % 4, y, z, k), at((x + 3) % 4, y, z, k)

    def pass_on(i, hk, n, device):
        return copy(gl.at[i, hk], gl.at[i, hk], ax_send.at[n], ax_recv.at[i, hk], device)

    def gather_own():
        for ph in (h, 1 - h):
            for pk in range(2):
                for away in range(8):
                    block = gl.at[xi, 2 * ph + pk, (y + 8 - away) % 8]
                    if away:
                        arrived(block, ay_recv.at[ph, pk, away])
                    else:

                        @pl.when(pk != k)
                        def _():
                            arrived(block, ay_recv.at[ph, pk, 0])

                pass_on(xi, 2 * ph + pk, 4 * pk + 2 * ph, right).start()
                pass_on(xi, 2 * ph + pk, 4 * pk + 2 * ph + 1, left).start()

    def gather_near(i, pk, device):
        for ph in (h, 1 - h):
            for which in range(2):
                arrived(gl.at[i, 2 * ph + which], ax_recv.at[i, 2 * ph + which])
                if which == pk:
                    pass_on(i, 2 * ph + which, 8 + ph, device).start()

    def gather_far(i):
        for hk in range(4):
            arrived(gl.at[i, hk], ax_recv.at[i, hk])

    def multiply(i):
        px = 2 * k + i
        for pk in range(2):
            acc = jnp.zeros((224, 256), F32)
            for hk in range(4):
                acc += lax.dot_general(
                    w[pk, :, 512 * hk : 512 * hk + 512], gl[i, hk].reshape(256, 512),
                    (((1,), (1,)), ((), ())), preferred_element_type=F32,
                )
            q[i, pk] = acc.astype(Z_TYPE)
            here = (c == px) & (k == pk)

            @pl.when(here)
            def _():
                z_in[c] = q[i, pk]

            @pl.when(jnp.logical_not(here))
            def _():
                copy(
                    q.at[i, pk], z_in.at[c], z_send.at[i, pk], z_recv.at[c], at(x, y, h * 4 + px, pk)
                ).start()

    sent(w.at[k], w_send)
    arrived(w.at[mate], w_recv)

    def near(i):
        rel = (2 * k + i - x + 4) % 4

        @pl.when(rel == 1)
        def _():
            gather_near(i, 1, left)

        @pl.when(rel == 3)
        def _():
            gather_near(i, 0, right)

    @pl.when(k == keeper)
    def _():
        gather_own()
        multiply(xi)
        near(1 - xi)
        multiply(1 - xi)

    @pl.when(k != keeper)
    def _():
        close = 1 - xi
        near(close)
        multiply(close)
        gather_far(1 - close)
        multiply(1 - close)

    for away in range(1, 4):
        pr = (row + 4 - away) % 4
        arrived(gram_in.at[pr], h_recv.at[away - 1])
    for r in range(4):
        gram_ref[:, 512 * r : 512 * r + 512] = gram_in[r]

    for away in range(4):
        pc = (c + away) % 4
        if away:
            arrived(z_in.at[pc], z_recv.at[pc])
        else:

            @pl.when(k != c // 2)
            def _():
                arrived(z_in.at[c], z_recv.at[c])

    prod_ref[...] = (
        z_in[0].astype(F32) + z_in[1].astype(F32) + z_in[2].astype(F32) + z_in[3].astype(F32)
    )

    for j in range(2):
        for direction in range(2):
            for step in range(3):
                sent(half(mine, j), ring_send.at[direction, step, j])
        sent(half(mine, j), ring_send.at[j, 3, j])
        for step in range(8):
            sent(half(mine, j), sib_send.at[step, j])
    for n in range(3):
        sent(part.at[n], x_send.at[n])
    for n in range(7):
        sent(s.at[0], y_send.at[n])
    sent(low.at[h], low_send)
    for n in range(3):
        sent(gram_in.at[0], h_send.at[n])
    for n in range(2):
        for away in range(1, 8):
            sent(low.at[0], ay_send.at[n, away])

        @pl.when(k != keeper)
        def _():
            sent(low.at[0], ay_send.at[n, 0])

    @pl.when(k == keeper)
    def _():
        for n in range(8):
            sent(gl.at[0, 0], ax_send.at[n])

    for n in range(2):
        sent(gl.at[0, 0], ax_send.at[8 + n])
    for i in range(2):
        for pk in range(2):
            here = (c == 2 * k + i) & (k == pk)

            @pl.when(jnp.logical_not(here))
            def _():
                sent(q.at[i, pk], z_send.at[i, pk])


def shards(grad_out, weight):
    dma = pltpu.SemaphoreType.DMA
    return pl.pallas_call(
        kernel,
        name="curvature",
        out_shape=(
            jax.ShapeDtypeStruct((8, 2048), F32),
            jax.ShapeDtypeStruct((224, 256), F32),
        ),
        in_specs=[pl.BlockSpec(memory_space=pl.ANY)] * 2,
        out_specs=(pl.BlockSpec(memory_space=pltpu.VMEM),) * 2,
        scratch_shapes=[
            pltpu.VMEM((1024, 512), BF16),
            pltpu.VMEM((16, 64, 1024), BF16),
            pltpu.VMEM((3, 256, 512), X_TYPE),
            pltpu.VMEM((256, 512), F32),
            pltpu.VMEM((3, 256, 512), X_TYPE),
            pltpu.VMEM((8, 32, 512), Y_TYPE),
            pltpu.VMEM((7, 32, 512), Y_TYPE),
            pltpu.VMEM((32, 512), F32),
            pltpu.VMEM((4, 8, 512), F32),
            pltpu.VMEM((2, 32, 512), BF16),
            pltpu.VMEM((2, 224, 2048), BF16),
            pltpu.VMEM((2, 4, 8, 32, 512), BF16),
            pltpu.VMEM((2, 2, 224, 256), Z_TYPE),
            pltpu.VMEM((4, 224, 256), Z_TYPE),
            dma((2,)),
            dma((2, 4, 2)), dma((2, 4, 2)),
            dma((8, 2)), dma((8, 2)),
            dma, dma,
            dma((3,)), dma((3,)),
            dma((7,)), dma((7,)),
            dma((3,)), dma((3,)),
            dma, dma,
            dma((2, 8)), dma((2, 2, 8)),
            dma((10,)), dma((2, 4)),
            dma((2, 2)), dma((4,)),
        ],
        compiler_params=pltpu.CompilerParams(
            collective_id=0, has_side_effects=True, vmem_limit_bytes=48 * 2**20
        ),
        cost_estimate=pl.CostEstimate(flops=2 * 10**9, bytes_accessed=3 * 2**20, transcendentals=0),
    )(grad_out, weight)


def solution(mesh):
    placed = (P("dp", ("col", "row")), P(("dp", "row"), "col"))
    return jax.shard_map(
        shards,
        mesh=mesh,
        in_specs=placed,
        out_specs=(P(("dp", "row"), "col"), P(("dp", "row"), "col")),
        check_vma=False,
    )
```

```python
import jax
import jax.numpy as jnp
from jax import lax
from jax.experimental import pallas as pl
from jax.experimental.pallas import tpu as pltpu
from jax.sharding import PartitionSpec as P

MESH = pl.DeviceIdType.MESH
F32, BF16 = jnp.float32, jnp.bfloat16
TOTAL = 32768
CH = 4
CW = 256
NQ = 4


def kernel(
    g_hbm, w_hbm, gram_ref, prod_ref,
    g, wt, pf, part, own, x_in, s, y_in, t, gram_in, low, w, gl, q, z_in,
    load_sem, swap_send, swap_recv, ring_send, ring_recv,
    x_send, x_recv, y_send, y_recv, h_send, h_recv, low_send, low_recv,
    ay_send, ay_recv, ax_send, ax_recv, fw_send, z_send, z_recv,
):
    dp, row, c = lax.axis_index("dp"), lax.axis_index("row"), lax.axis_index("col")
    x, y, h, k = dp // 8, dp % 8, row // 2, row % 2
    z = h * 4 + c

    def at(px, py, pz, pk):
        return (px * 8 + py, (pz // 4) * 2 + pk, pz % 4)

    def copy(src, dst, send, recv, device):
        return pltpu.make_async_remote_copy(
            src_ref=src, dst_ref=dst, send_sem=send, recv_sem=recv,
            device_id=device, device_id_type=MESH,
        )

    sibling = at(x, y, z, 1 - k)
    opposite = at(x, y, (z + 4) % 8, k)
    right, left = at((x + 1) % 4, y, z, k), at((x + 3) % 4, y, z, k)

    def arrived(dst, recv):
        copy(dst, dst, recv, recv, sibling).wait_recv()

    def sent(src, send):
        copy(src, src, send, send, sibling).wait_send()

    load_g = pltpu.make_async_copy(g_hbm, g.at[k], load_sem.at[0])
    load_w = pltpu.make_async_copy(w_hbm, w.at[k], load_sem.at[1])
    load_g.start()
    load_w.start()

    barrier = pltpu.get_barrier_semaphore()
    partners = [sibling]
    partners += [at((x + i) % 4, y, z, k) for i in range(1, 4)]
    partners += [at(x, (y + i) % 8, z, k) for i in range(1, 8)]
    partners += [at(x, y, (z + i) % 8, k) for i in range(1, 8)]
    partners += [at(x, y, h * 4 + (c + i) % 4, 1 - k) for i in range(1, 4)]
    for partner in partners:
        pl.semaphore_signal(barrier, inc=1, device_id=partner, device_id_type=MESH)

    def slot(pz):
        return (pz % 4) * 2 + pz // 4

    def piece(b, j):
        return wt.at[b, pl.ds(16 * j, 16)]

    load_g.wait()
    mine = slot(z)
    wt[mine] = g[k, :, :128].astype(F32).T[:64].astype(BF16)
    load_w.wait()
    pl.semaphore_wait(barrier, len(partners))

    to = (at(x, y, (z + 1) % 8, k), at(x, y, (z + 7) % 8, k))

    def ring(direction, b, step, j):
        return copy(
            piece(b, j), piece(b, j), ring_send.at[direction, step, j],
            ring_recv.at[direction, step, j], to[direction],
        )

    for j in range(NQ):
        ring(0, mine, 0, j).start()
        ring(1, mine, 0, j).start()
    copy(g.at[k], g.at[k], swap_send.at[0], swap_recv.at[0], sibling).start()
    copy(w.at[k], w.at[k], swap_send.at[1], swap_recv.at[1], sibling).start()
    for step in range(1, 4):
        for j in range(NQ):
            for direction in range(2):
                away = step if direction == 1 else 8 - step
                b = slot((z + away) % 8)
                arrived(piece(b, j), ring_recv.at[direction, step - 1, j])
                if step < 3 or direction == j // (NQ // 2):
                    ring(direction, b, step, j).start()
    far = slot((z + 4) % 8)
    for j in range(NQ):
        arrived(piece(far, j), ring_recv.at[j // (NQ // 2), 3, j])
    arrived(g.at[1 - k], swap_recv.at[0])

    def form(n):
        got = jnp.dot(
            wt[...].reshape(512, 1024), g[n // 2, :, CW * (n % 2) : CW * (n % 2) + CW],
            preferred_element_type=F32,
        )
        for px in range(4):
            for py in range(8):
                for ph in range(2):
                    a = 128 * px + 64 * ph + 8 * py
                    b = 16 * py + 8 * ph
                    pf[px, b : b + 8] = got[a : a + 8]
        for away in (2, 1, 3):
            px = (x + away) % 4
            part[n, away - 1] = pf[px].astype(BF16)
            copy(
                part.at[n, away - 1], x_in.at[n, away - 1],
                x_send.at[n, away - 1], x_recv.at[n, away - 1], at(px, y, z, k),
            ).start()
        own[n] = pf[x]

    def sum_x(n):
        for away in (1, 3, 2):
            arrived(x_in.at[n, away - 1], x_recv.at[n, away - 1])
        terms = x_in[n, 0].astype(F32) + x_in[n, 1].astype(F32) + x_in[n, 2].astype(F32)
        s[n] = (own[n] + terms).reshape(8, 16, CW)
        for away in (4, 3, 5, 2, 6, 1, 7):
            copy(
                s.at[n, (y + away) % 8], y_in.at[n, away - 1],
                y_send.at[n, away - 1], y_recv.at[n, away - 1], at(x, (y + away) % 8, z, k),
            ).start()

    def spread(ph, n):
        for away in (4, 3, 5, 2, 6, 1, 7):
            copy(
                low.at[ph, n], gl.at[x, ph, n, y], ay_send.at[ph, n, away - 1],
                ay_recv.at[ph, n, away - 1], at(x, (y + away) % 8, z, k),
            ).start()
        gl[x, ph, n, y] = low[ph, n]

    def sum_y(n):
        total = s[n, y]
        for away in (1, 7, 2, 6, 3, 5, 4):
            arrived(y_in.at[n, away - 1], y_recv.at[n, away - 1])
            total += y_in[n, away - 1]
        total = total * (1.0 / TOTAL)
        low[h, n] = total.astype(BF16)
        copy(low.at[h, n], low.at[h, n], low_send.at[n], low_recv.at[n], opposite).start()
        spread(h, n)
        t[n] = total
        copy(
            t.at[n, pl.ds(pl.multiple_of(8 * (1 - h), 8), 8)], gram_in.at[h, n],
            h_send.at[n], h_recv.at[n], opposite,
        ).start()
        gram_in[h, n] = t[n, pl.ds(pl.multiple_of(8 * h, 8), 8)]

    def spread_other(n):
        arrived(low.at[1 - h, n], low_recv.at[n])
        spread(1 - h, n)

    def pass_on(px, ph, n, send, recv, device):
        return copy(gl.at[px, ph, n], gl.at[px, ph, n], send, recv, device)

    def send_own(ph, n):
        for away in (1, 7, 2, 6, 3, 5, 4):
            arrived(gl.at[x, ph, n, (y + 8 - away) % 8], ay_recv.at[ph, n, away - 1])
        pass_on(x, ph, n, ax_send.at[0, ph, n], ax_recv.at[0, ph, n], right).start()
        pass_on(x, ph, n, ax_send.at[1, ph, n], ax_recv.at[1, ph, n], left).start()

    def send_near(ph, n):
        arrived(gl.at[(x + 3) % 4, ph, n], ax_recv.at[0, ph, n])
        if n < CH // 2:
            pass_on((x + 3) % 4, ph, n, fw_send.at[ph, n], ax_recv.at[2, ph, n], right).start()
        arrived(gl.at[(x + 1) % 4, ph, n], ax_recv.at[1, ph, n])
        if n >= CH // 2:
            pass_on((x + 1) % 4, ph, n, fw_send.at[ph, n], ax_recv.at[2, ph, n], left).start()

    def run(stage, n):
        if 0 <= n < CH:
            stage(n)

    for n in range(CH):
        form(n)
    for n in range(CH + 4):
        run(sum_x, n)
        run(sum_y, n - 1)
        run(lambda m: send_own(h, m), n - 2)
        run(spread_other, n - 2)
        run(lambda m: send_own(1 - h, m), n - 3)
        run(lambda m: send_near(h, m), n - 3)
        run(lambda m: send_near(1 - h, m), n - 4)

    def multiply(away):
        px = (x + away) % 4
        acc = jnp.zeros((448, 128), F32)
        for ph in range(2):
            for n in range(CH):
                a = 1024 * ph + CW * n
                acc += lax.dot_general(
                    w[:, :, a : a + CW].reshape(448, CW), gl[px, ph, n].reshape(128, CW),
                    (((1,), (1,)), ((), ())), preferred_element_type=F32,
                )
        q[away] = acc.astype(BF16).reshape(2, 224, 128)
        for pk in range(2):
            here = (c == px) & (k == pk)

            @pl.when(here)
            def _():
                z_in[c, k] = q[away, pk]

            @pl.when(jnp.logical_not(here))
            def _():
                copy(
                    q.at[away, pk], z_in.at[c, k], z_send.at[away, pk], z_recv.at[c, k],
                    at(x, y, h * 4 + px, pk),
                ).start()

    arrived(w.at[1 - k], swap_recv.at[1])
    multiply(0)
    multiply(1)
    multiply(3)
    for ph in range(2):
        for n in range(CH):
            arrived(gl.at[(x + 2) % 4, ph, n], ax_recv.at[2, ph, n])
    multiply(2)

    for n in range(CH):
        arrived(gram_in.at[1 - h, n], h_recv.at[n])
    for ph in range(2):
        for n in range(CH):
            a = 1024 * ph + CW * n
            gram_ref[:, a : a + CW] = gram_in[ph, n]

    for away in range(1, 4):
        for pk in range(2):
            pc = (c + away) % 4
            arrived(z_in.at[pc, pk], z_recv.at[pc, pk])
    arrived(z_in.at[c, 1 - k], z_recv.at[c, 1 - k])
    acc = jnp.zeros((224, 256), F32)
    source = lax.broadcasted_iota(jnp.int32, (128, 256), 0)
    target = lax.broadcasted_iota(jnp.int32, (128, 256), 1)
    for pk in range(2):
        place = (target == (source // 8) * 16 + 8 * pk + source % 8).astype(F32).astype(BF16)
        for pc in range(4):
            acc += jnp.dot(z_in[pc, pk], place, preferred_element_type=F32)
    prod_ref[...] = acc

    for j in range(NQ):
        for direction in range(2):
            for step in range(3):
                sent(piece(mine, j), ring_send.at[direction, step, j])
        sent(piece(mine, j), ring_send.at[j // (NQ // 2), 3, j])
    sent(g.at[k], swap_send.at[0])
    sent(w.at[k], swap_send.at[1])
    for n in range(CH):
        for away in range(3):
            sent(part.at[n, away], x_send.at[n, away])
        for away in range(7):
            sent(s.at[n, 0], y_send.at[n, away])
        sent(low.at[h, n], low_send.at[n])
        sent(gram_in.at[0, n], h_send.at[n])
        for ph in range(2):
            for away in range(7):
                sent(low.at[ph, n], ay_send.at[ph, n, away])
            for side in range(2):
                sent(gl.at[x, ph, n], ax_send.at[side, ph, n])
            sent(gl.at[x, ph, n], fw_send.at[ph, n])
    for away in range(4):
        for pk in range(2):

            @pl.when(jnp.logical_not((c == (x + away) % 4) & (k == pk)))
            def _():
                sent(q.at[away, pk], z_send.at[away, pk])


def shards(grad_out, weight):
    dma = pltpu.SemaphoreType.DMA
    return pl.pallas_call(
        kernel,
        name="curvature",
        out_shape=(
            jax.ShapeDtypeStruct((8, 2048), F32),
            jax.ShapeDtypeStruct((224, 256), F32),
        ),
        in_specs=[pl.BlockSpec(memory_space=pltpu.HBM)] * 2,
        out_specs=(pl.BlockSpec(memory_space=pltpu.VMEM),) * 2,
        scratch_shapes=[
            pltpu.VMEM((2, 1024, 512), BF16),
            pltpu.VMEM((8, 64, 1024), BF16),
            pltpu.VMEM((4, 128, CW), F32),
            pltpu.VMEM((CH, 3, 128, CW), BF16),
            pltpu.VMEM((CH, 128, CW), F32),
            pltpu.VMEM((CH, 3, 128, CW), BF16),
            pltpu.VMEM((CH, 8, 16, CW), F32),
            pltpu.VMEM((CH, 7, 16, CW), F32),
            pltpu.VMEM((CH, 16, CW), F32),
            pltpu.VMEM((2, CH, 8, CW), F32),
            pltpu.VMEM((2, CH, 16, CW), BF16),
            pltpu.VMEM((2, 224, 2048), BF16),
            pltpu.VMEM((4, 2, CH, 8, 16, CW), BF16),
            pltpu.VMEM((4, 2, 224, 128), BF16),
            pltpu.VMEM((4, 2, 224, 128), BF16),
            dma((2,)),
            dma((2,)), dma((2,)),
            dma((2, 4, NQ)), dma((2, 4, NQ)),
            dma((CH, 3)), dma((CH, 3)),
            dma((CH, 7)), dma((CH, 7)),
            dma((CH,)), dma((CH,)),
            dma((CH,)), dma((CH,)),
            dma((2, CH, 7)), dma((2, CH, 7)),
            dma((2, 2, CH)), dma((3, 2, CH)), dma((2, CH)),
            dma((4, 2)), dma((4, 2)),
        ],
        compiler_params=pltpu.CompilerParams(
            collective_id=0, has_side_effects=True, vmem_limit_bytes=48 * 2**20
        ),
        cost_estimate=pl.CostEstimate(flops=2 * 10**9, bytes_accessed=3 * 2**20, transcendentals=0),
    )(grad_out, weight)


def solution(mesh):
    placed = (P("dp", ("col", "row")), P(("dp", "row"), "col"))
    return jax.shard_map(
        shards,
        mesh=mesh,
        in_specs=placed,
        out_specs=(P(("dp", "row"), "col"), P(("dp", "row"), "col")),
        check_vma=False,
    )
```

```python
import jax
import jax.numpy as jnp
from jax import lax
from jax.experimental import pallas as pl
from jax.experimental.pallas import tpu as pltpu
from jax.sharding import PartitionSpec as P

MESH = pl.DeviceIdType.MESH
F32, BF16 = jnp.float32, jnp.bfloat16
TOTAL = 32768
CH = 4
CW = 1024 // CH
U = 256 // CW
NQ = 4
LAG_Y, LAG_OWN, LAG_H, LAG_OWN2, LAG_NEAR, LAG_NEAR2, LAG_FAR, LAG_FAR2 = 1, 2, 2, 3, 3, 4, 4, 5


def kernel(
    g_hbm, w_hbm, gram_ref, prod_ref,
    win, g, wt, place, pf, part, own, x_in, s, y_in, t, gram_in, low, w, gl, acc, q, z_in,
    load_sem, swap_send, swap_recv, ring_send, ring_recv,
    x_send, x_recv, y_send, y_recv, h_send, h_recv, low_send, low_recv,
    ay_send, ay_recv, ax_send, ax_recv, fw_send, z_send, z_recv,
):
    dp, row, c = lax.axis_index("dp"), lax.axis_index("row"), lax.axis_index("col")
    x, y, h, k = dp // 8, dp % 8, row // 2, row % 2
    z = h * 4 + c

    xs = [x] + [(x + i) % 4 for i in range(1, 4)]
    ys = [y] + [(y + i) % 8 for i in range(1, 8)]

    def at(px, py, pz, pk):
        return (px * 8 + py, (pz // 4) * 2 + pk, pz % 4)

    def copy(src, dst, send, recv, device):
        return pltpu.make_async_remote_copy(
            src_ref=src, dst_ref=dst, send_sem=send, recv_sem=recv,
            device_id=device, device_id_type=MESH,
        )

    sibling = at(x, y, z, 1 - k)
    opposite = at(x, y, (z + 4) % 8, k)
    right, left = at(xs[1], y, z, k), at(xs[3], y, z, k)

    def arrived(dst, recv):
        copy(dst, dst, recv, recv, sibling).wait_recv()

    def sent(src, send):
        copy(src, src, send, send, sibling).wait_send()

    load_g = pltpu.make_async_copy(g_hbm, g.at[k], load_sem.at[0])
    load_w = pltpu.make_async_copy(w_hbm, w.at[k], load_sem.at[1])
    load_win = pltpu.make_async_copy(g_hbm.at[:, pl.ds(0, 128)], win, load_sem.at[2])
    load_win.start()
    load_g.start()
    load_w.start()

    barrier = pltpu.get_barrier_semaphore()
    partners = [sibling]
    partners += [at(xs[i], y, z, k) for i in range(1, 4)]
    partners += [at(x, ys[i], z, k) for i in range(1, 8)]
    partners += [at(x, y, (z + i) % 8, k) for i in range(1, 8)]
    partners += [at(x, y, h * 4 + (c + i) % 4, 1 - k) for i in range(1, 4)]
    for partner in partners:
        pl.semaphore_signal(barrier, inc=1, device_id=partner, device_id_type=MESH)

    def slot(pz):
        return (pz % 4) * 2 + pz // 4

    def piece(b, j):
        return wt.at[b, pl.ds(16 * j, 16)]

    mine = slot(z)
    line = lax.broadcasted_iota(jnp.int32, (64, 128), 0)
    lane = lax.broadcasted_iota(jnp.int32, (64, 128), 1)
    pick = (line == lane).astype(F32).astype(BF16)
    load_win.wait()
    wt[mine] = lax.dot_general(
        pick, win[...], (((1,), (1,)), ((), ())), preferred_element_type=F32
    ).astype(BF16)
    pl.semaphore_wait(barrier, len(partners))

    to = (at(x, y, (z + 1) % 8, k), at(x, y, (z + 7) % 8, k))

    def ring(direction, b, step, j):
        return copy(
            piece(b, j), piece(b, j), ring_send,
            ring_recv.at[direction, step, j], to[direction],
        )

    for j in range(NQ):
        ring(0, mine, 0, j).start()
        ring(1, mine, 0, j).start()
    load_g.wait()
    copy(g.at[k], g.at[k], swap_send.at[0], swap_recv.at[0], sibling).start()
    load_w.wait()
    copy(w.at[k], w.at[k], swap_send.at[1], swap_recv.at[1], sibling).start()
    source = lax.broadcasted_iota(jnp.int32, (128, 256), 0)
    target = lax.broadcasted_iota(jnp.int32, (128, 256), 1)
    for pk in range(2):
        place[pk] = (target == (source // 8) * 16 + 8 * pk + source % 8).astype(F32).astype(BF16)
    for step in range(1, 4):
        for j in range(NQ):
            for direction in range(2):
                away = step if direction == 1 else 8 - step
                b = slot((z + away) % 8)
                arrived(piece(b, j), ring_recv.at[direction, step - 1, j])
                if step < 3 or direction == j // (NQ // 2):
                    ring(direction, b, step, j).start()
    far = slot((z + 4) % 8)
    for j in range(NQ):
        arrived(piece(far, j), ring_recv.at[j // (NQ // 2), 3, j])
    arrived(g.at[1 - k], swap_recv.at[0])

    def form(m):
        got = jnp.dot(
            wt[...].reshape(512, 1024), g[m // 2, :, 256 * (m % 2) : 256 * (m % 2) + 256],
            preferred_element_type=F32,
        )
        for u in range(U):
            for px in range(4):
                for py in range(8):
                    for ph in range(2):
                        a = 128 * px + 64 * ph + 8 * py
                        b = 16 * py + 8 * ph
                        pf[u, px, b : b + 8] = got[a : a + 8, CW * u : CW * u + CW]
        for u in range(U):
            n = U * m + u
            for away in (2, 1, 3):
                px = xs[away]
                part[n, away - 1] = pf[u, px].astype(BF16)
                copy(
                    part.at[n, away - 1], x_in.at[n, away - 1],
                    x_send, x_recv.at[n], at(px, y, z, k),
                ).start()
            own[n] = pf[u, x]

    def sum_x(n):
        arrived(x_in.at[n], x_recv.at[n])
        terms = x_in[n, 0].astype(F32) + x_in[n, 1].astype(F32) + x_in[n, 2].astype(F32)
        s[n] = (own[n] + terms).reshape(8, 16, CW)
        for away in (4, 3, 5, 2, 6, 1, 7):
            copy(
                s.at[n, ys[away]], y_in.at[n, away - 1],
                y_send, y_recv.at[n], at(x, ys[away], z, k),
            ).start()

    def spread(ph, n):
        for away in (4, 3, 5, 2, 6, 1, 7):
            copy(
                low.at[ph, n], gl.at[x, ph, n, y], ay_send,
                ay_recv.at[ph, n], at(x, ys[away], z, k),
            ).start()
        gl[x, ph, n, y] = low[ph, n]

    def sum_y(n):
        arrived(y_in.at[n], y_recv.at[n])
        total = s[n, y]
        for away in range(7):
            total += y_in[n, away]
        total = total * (1.0 / TOTAL)
        low[h, n] = total.astype(BF16)
        copy(low.at[h, n], low.at[h, n], low_send, low_recv.at[n], opposite).start()
        spread(h, n)
        t[n] = total
        copy(
            t.at[n, pl.ds(pl.multiple_of(8 * (1 - h), 8), 8)], gram_in.at[h, n],
            h_send, h_recv.at[n], opposite,
        ).start()
        gram_in[h, n] = t[n, pl.ds(pl.multiple_of(8 * h, 8), 8)]

    def spread_other(n):
        arrived(low.at[1 - h, n], low_recv.at[n])
        spread(1 - h, n)

    def pass_on(px, ph, n, send, recv, device):
        return copy(gl.at[px, ph, n], gl.at[px, ph, n], send, recv, device)

    def send_own(ph, n):
        arrived(gl.at[x, ph, n, pl.ds(0, 7)], ay_recv.at[ph, n])
        pass_on(x, ph, n, ax_send, ax_recv.at[0, ph, n], right).start()
        pass_on(x, ph, n, ax_send, ax_recv.at[1, ph, n], left).start()

    def send_near(ph, n):
        arrived(gl.at[xs[3], ph, n], ax_recv.at[0, ph, n])
        if n < CH // 2:
            pass_on(xs[3], ph, n, fw_send, ax_recv.at[2, ph, n], right).start()
        arrived(gl.at[xs[1], ph, n], ax_recv.at[1, ph, n])
        if n >= CH // 2:
            pass_on(xs[1], ph, n, fw_send, ax_recv.at[2, ph, n], left).start()

    def last(ph, n):
        arrived(gl.at[xs[2], ph, n], ax_recv.at[2, ph, n])

    def multiply(away, ph, n):
        if (n + 1) % U:
            return
        a = 1024 * ph + CW * (n + 1 - U)
        px = xs[away]
        low_rows = jnp.concatenate(
            [gl[px, ph, n + 1 - U + u].reshape(128, CW) for u in range(U)], axis=1
        )
        acc[away] += lax.dot_general(
            w[:, :, pl.ds(a, 256)].reshape(448, 256), low_rows,
            (((1,), (1,)), ((), ())), preferred_element_type=F32,
        )

    def give(away):
        px = xs[away]
        q[away] = acc[away].astype(BF16).reshape(2, 224, 128)
        for pk in range(2):
            here = (c == px) & (k == pk)

            @pl.when(here)
            def _():
                z_in[c, k] = q[away, pk]

            @pl.when(jnp.logical_not(here))
            def _():
                copy(
                    q.at[away, pk], z_in.at[c, k], z_send.at[away, pk], z_recv.at[c, k],
                    at(x, y, h * 4 + px, pk),
                ).start()

    def own_step(ph, n):
        send_own(ph, n)
        multiply(0, ph, n)

    def near_step(ph, n):
        send_near(ph, n)
        multiply(1, ph, n)
        multiply(3, ph, n)

    def last_step(ph, n):
        last(ph, n)
        multiply(2, ph, n)

    def run(stage, *args):
        if 0 <= args[-1] < CH:
            stage(*args)

    for m in range(CH // U):
        form(m)
    acc[...] = jnp.zeros_like(acc)
    arrived(w.at[1 - k], swap_recv.at[1])
    for n in range(CH + LAG_FAR2):
        run(sum_x, n)
        run(sum_y, n - LAG_Y)
        run(own_step, h, n - LAG_OWN)
        run(spread_other, n - LAG_H)
        run(own_step, 1 - h, n - LAG_OWN2)
        if n - LAG_OWN2 == CH - 1:
            give(0)
        run(near_step, h, n - LAG_NEAR)
        run(near_step, 1 - h, n - LAG_NEAR2)
        if n - LAG_NEAR2 == CH - 1:
            give(1)
            give(3)
        run(last_step, h, n - LAG_FAR)
        run(last_step, 1 - h, n - LAG_FAR2)
    give(2)

    for n in range(CH):
        arrived(gram_in.at[1 - h, n], h_recv.at[n])
    for ph in range(2):
        for n in range(CH):
            a = 1024 * ph + CW * n
            gram_ref[:, a : a + CW] = gram_in[ph, n]

    sent(wt.at[pl.ds(0, 7)], ring_send)
    sent(g.at[k], swap_send.at[0])
    sent(w.at[k], swap_send.at[1])
    sent(part, x_send)
    sent(y_in, y_send)
    sent(low.at[h], low_send)
    sent(gram_in.at[h], h_send)
    sent(gl.at[0, :, :, pl.ds(0, 7)], ay_send)
    sent(gl.at[pl.ds(0, 2)], ax_send)
    sent(gl.at[0], fw_send)

    for away in range(1, 4):
        for pk in range(2):
            pc = (c + away) % 4
            arrived(z_in.at[pc, pk], z_recv.at[pc, pk])
    arrived(z_in.at[c, 1 - k], z_recv.at[c, 1 - k])
    total = jnp.zeros((224, 256), F32)
    for pk in range(2):
        for pc in range(4):
            total += jnp.dot(z_in[pc, pk], place[pk], preferred_element_type=F32)
    prod_ref[...] = total

    for away in range(4):
        for pk in range(2):

            @pl.when(jnp.logical_not((c == (x + away) % 4) & (k == pk)))
            def _():
                sent(q.at[away, pk], z_send.at[away, pk])


def shards(grad_out, weight):
    dma = pltpu.SemaphoreType.DMA
    return pl.pallas_call(
        kernel,
        name="curvature",
        out_shape=(
            jax.ShapeDtypeStruct((8, 2048), F32),
            jax.ShapeDtypeStruct((224, 256), F32),
        ),
        in_specs=[pl.BlockSpec(memory_space=pltpu.HBM)] * 2,
        out_specs=(pl.BlockSpec(memory_space=pltpu.VMEM),) * 2,
        scratch_shapes=[
            pltpu.VMEM((1024, 128), BF16),
            pltpu.VMEM((2, 1024, 512), BF16),
            pltpu.VMEM((8, 64, 1024), BF16),
            pltpu.VMEM((2, 128, 256), BF16),
            pltpu.VMEM((U, 4, 128, CW), F32),
            pltpu.VMEM((CH, 3, 128, CW), BF16),
            pltpu.VMEM((CH, 128, CW), F32),
            pltpu.VMEM((CH, 3, 128, CW), BF16),
            pltpu.VMEM((CH, 8, 16, CW), F32),
            pltpu.VMEM((CH, 7, 16, CW), F32),
            pltpu.VMEM((CH, 16, CW), F32),
            pltpu.VMEM((2, CH, 8, CW), F32),
            pltpu.VMEM((2, CH, 16, CW), BF16),
            pltpu.VMEM((2, 224, 2048), BF16),
            pltpu.VMEM((4, 2, CH, 8, 16, CW), BF16),
            pltpu.VMEM((4, 448, 128), F32),
            pltpu.VMEM((4, 2, 224, 128), BF16),
            pltpu.VMEM((4, 2, 224, 128), BF16),
            dma((3,)),
            dma((2,)), dma((2,)),
            dma, dma((2, 4, NQ)),
            dma, dma((CH,)),
            dma, dma((CH,)),
            dma, dma((CH,)),
            dma, dma((CH,)),
            dma, dma((2, CH)),
            dma, dma((3, 2, CH)), dma,
            dma((4, 2)), dma((4, 2)),
        ],
        compiler_params=pltpu.CompilerParams(
            collective_id=0, has_side_effects=True, vmem_limit_bytes=53 * 2**20
        ),
        cost_estimate=pl.CostEstimate(flops=2 * 10**9, bytes_accessed=3 * 2**20, transcendentals=0),
    )(grad_out, weight)


def solution(mesh):
    placed = (P("dp", ("col", "row")), P(("dp", "row"), "col"))
    return jax.shard_map(
        shards,
        mesh=mesh,
        in_specs=placed,
        out_specs=(P(("dp", "row"), "col"), P(("dp", "row"), "col")),
        check_vma=False,
    )
```

```python
import jax
import jax.numpy as jnp
from jax import lax
from jax.experimental import pallas as pl
from jax.experimental.pallas import tpu as pltpu
from jax.sharding import PartitionSpec as P

MESH = pl.DeviceIdType.MESH
F32, BF16 = jnp.float32, jnp.bfloat16
TOTAL = 32768
CW = 128
CH = 8
PARTS = ((0, 2), (2, 2), (4, 2), (6, 2))
NP = len(PARTS)
NQ = 4
LAG_Y, LAG_OWN, LAG_H, LAG_OWN2, LAG_NEAR, LAG_NEAR2, LAG_FAR, LAG_FAR2 = 1, 2, 2, 3, 3, 4, 5, 5


def kernel(
    g_hbm, w_hbm, gram_ref, prod_ref,
    win, g, wt, place, pf, part, own, x_in, s, y_in, t, gram_in, low, w, gl, acc, q, z_in,
    load_sem, swap_send, swap_recv, ring_send, ring_recv,
    x_send, x_recv, y_send, y_recv, h_send, h_recv, low_send, low_recv,
    ay_send, ay_recv, ax_send, ax_recv, fw_send, z_send, z_recv,
):
    dp, row, c = lax.axis_index("dp"), lax.axis_index("row"), lax.axis_index("col")
    x, y, h, k = dp // 8, dp % 8, row // 2, row % 2
    z = h * 4 + c

    xs = [x] + [(x + i) % 4 for i in range(1, 4)]
    ys = [y] + [(y + i) % 8 for i in range(1, 8)]

    def at(px, py, pz, pk):
        return (px * 8 + py, (pz // 4) * 2 + pk, pz % 4)

    def copy(src, dst, send, recv, device):
        return pltpu.make_async_remote_copy(
            src_ref=src, dst_ref=dst, send_sem=send, recv_sem=recv,
            device_id=device, device_id_type=MESH,
        )

    sibling = at(x, y, z, 1 - k)
    opposite = at(x, y, (z + 4) % 8, k)
    right, left = at(xs[1], y, z, k), at(xs[3], y, z, k)

    def arrived(dst, recv):
        copy(dst, dst, recv, recv, sibling).wait_recv()

    def sent(src, send):
        copy(src, src, send, send, sibling).wait_send()

    load_g = pltpu.make_async_copy(g_hbm, g.at[k], load_sem.at[0])
    load_w = pltpu.make_async_copy(w_hbm, w.at[k], load_sem.at[1])
    load_win = pltpu.make_async_copy(g_hbm.at[:, pl.ds(0, 128)], win, load_sem.at[2])
    load_win.start()
    load_g.start()
    load_w.start()

    barrier = pltpu.get_barrier_semaphore()
    partners = [sibling]
    partners += [at(xs[i], y, z, k) for i in range(1, 4)]
    partners += [at(x, ys[i], z, k) for i in range(1, 8)]
    partners += [at(x, y, (z + i) % 8, k) for i in range(1, 8)]
    partners += [at(x, y, h * 4 + (c + i) % 4, 1 - k) for i in range(1, 4)]
    for partner in partners:
        pl.semaphore_signal(barrier, inc=1, device_id=partner, device_id_type=MESH)

    def slot(pz):
        return (pz % 4) * 2 + pz // 4

    def piece(b, j):
        return wt.at[b, pl.ds(16 * j, 16)]

    mine = slot(z)
    line = lax.broadcasted_iota(jnp.int32, (64, 128), 0)
    lane = lax.broadcasted_iota(jnp.int32, (64, 128), 1)
    pick = (line == lane).astype(F32).astype(BF16)
    load_win.wait()
    wt[mine] = lax.dot_general(
        pick, win[...], (((1,), (1,)), ((), ())), preferred_element_type=F32
    ).astype(BF16)
    pl.semaphore_wait(barrier, len(partners))

    to = (at(x, y, (z + 1) % 8, k), at(x, y, (z + 7) % 8, k))

    def ring(direction, b, step, j):
        return copy(
            piece(b, j), piece(b, j), ring_send,
            ring_recv.at[direction, step, j], to[direction],
        )

    for j in range(NQ):
        ring(0, mine, 0, j).start()
        ring(1, mine, 0, j).start()
    load_g.wait()
    copy(g.at[k], g.at[k], swap_send.at[0], swap_recv.at[0], sibling).start()
    load_w.wait()
    copy(w.at[k], w.at[k], swap_send.at[1], swap_recv.at[1], sibling).start()
    source = lax.broadcasted_iota(jnp.int32, (128, 256), 0)
    target = lax.broadcasted_iota(jnp.int32, (128, 256), 1)
    for pk in range(2):
        place[pk] = (target == (source // 8) * 16 + 8 * pk + source % 8).astype(F32).astype(BF16)
    for step in range(1, 4):
        for j in range(NQ):
            for direction in range(2):
                away = step if direction == 1 else 8 - step
                b = slot((z + away) % 8)
                arrived(piece(b, j), ring_recv.at[direction, step - 1, j])
                if step < 3 or direction == j // (NQ // 2):
                    ring(direction, b, step, j).start()
    far = slot((z + 4) % 8)
    for j in range(NQ):
        arrived(piece(far, j), ring_recv.at[j // (NQ // 2), 3, j])
    arrived(g.at[1 - k], swap_recv.at[0])

    def form(m):
        got = jnp.dot(
            wt[...].reshape(512, 1024), g[m // 2, :, 256 * (m % 2) : 256 * (m % 2) + 256],
            preferred_element_type=F32,
        )
        for u in range(2):
            for px in range(4):
                for py in range(8):
                    for ph in range(2):
                        a = 128 * px + 64 * ph + 8 * py
                        b = 16 * py + 8 * ph
                        pf[u, px, b : b + 8] = got[a : a + 8, CW * u : CW * u + CW]
        for i in range(2):
            for away in (2, 1, 3):
                part[2 * m + i, away - 1] = pf[i, xs[away]].astype(BF16)
            own[2 * m + i] = pf[i, x]
        for p, (n, units) in enumerate(PARTS):
            if (n + units - 1) // 2 == m:
                here = pl.ds(n, units)
                for away in (2, 1, 3):
                    copy(
                        part.at[here, away - 1], x_in.at[here, away - 1],
                        x_send, x_recv.at[p], at(xs[away], y, z, k),
                    ).start()

    def sum_x(p):
        first, units = PARTS[p]
        here = pl.ds(first, units)
        arrived(x_in.at[here], x_recv.at[p])
        for n in range(first, first + units):
            terms = x_in[n, 0].astype(F32) + x_in[n, 1].astype(F32) + x_in[n, 2].astype(F32)
            s[n] = (own[n] + terms).reshape(8, 16, CW)
        for away in (4, 3, 5, 2, 6, 1, 7):
            copy(
                s.at[here, ys[away]], y_in.at[here, away - 1], y_send, y_recv.at[p],
                at(x, ys[away], z, k),
            ).start()

    def spread(ph, p):
        here = pl.ds(*PARTS[p])
        for away in (4, 3, 5, 2, 6, 1, 7):
            copy(
                low.at[ph, here], gl.at[x, ph, here, y], ay_send, ay_recv.at[ph, p],
                at(x, ys[away], z, k),
            ).start()
        for n in range(PARTS[p][0], sum(PARTS[p])):
            gl[x, ph, n, y] = low[ph, n]

    def sum_y(p):
        first, units = PARTS[p]
        here = pl.ds(first, units)
        arrived(y_in.at[here], y_recv.at[p])
        for n in range(first, first + units):
            total = s[n, y]
            for away in range(7):
                total += y_in[n, away]
            total = total * (1.0 / TOTAL)
            low[h, n] = total.astype(BF16)
            t[n] = total
        copy(low.at[h, here], low.at[h, here], low_send, low_recv.at[p], opposite).start()
        spread(h, p)
        copy(
            t.at[here, pl.ds(pl.multiple_of(8 * (1 - h), 8), 8)], gram_in.at[h, here],
            h_send, h_recv.at[p], opposite,
        ).start()
        for n in range(first, first + units):
            gram_in[h, n] = t[n, pl.ds(pl.multiple_of(8 * h, 8), 8)]

    def spread_other(p):
        arrived(low.at[1 - h, pl.ds(*PARTS[p])], low_recv.at[p])
        spread(1 - h, p)

    def pass_on(px, ph, p, send, recv, device):
        here = pl.ds(*PARTS[p])
        return copy(gl.at[px, ph, here], gl.at[px, ph, here], send, recv, device)

    def send_own(ph, p):
        arrived(gl.at[x, ph, pl.ds(*PARTS[p]), pl.ds(0, 7)], ay_recv.at[ph, p])
        pass_on(x, ph, p, ax_send, ax_recv.at[0, ph, p], right).start()
        pass_on(x, ph, p, ax_send, ax_recv.at[1, ph, p], left).start()

    def send_near(ph, p, other):
        here = pl.ds(*PARTS[p])
        arrived(gl.at[xs[3], ph, here], ax_recv.at[0, ph, p])
        if not other:
            pass_on(xs[3], ph, p, fw_send, ax_recv.at[2, ph, p], right).start()
        arrived(gl.at[xs[1], ph, here], ax_recv.at[1, ph, p])
        if other:
            pass_on(xs[1], ph, p, fw_send, ax_recv.at[2, ph, p], left).start()

    def last(ph, p):
        arrived(gl.at[xs[2], ph, pl.ds(*PARTS[p])], ax_recv.at[2, ph, p])

    def multiply(away, ph, p):
        px = xs[away]
        for n in range(PARTS[p][0] // 2 * 2, sum(PARTS[p]) // 2 * 2, 2):
            a = 1024 * ph + CW * n
            low_rows = jnp.concatenate(
                [gl[px, ph, n].reshape(128, CW), gl[px, ph, n + 1].reshape(128, CW)], axis=1
            )
            acc[away] += lax.dot_general(
                w[:, :, pl.ds(a, 256)].reshape(448, 256), low_rows,
                (((1,), (1,)), ((), ())), preferred_element_type=F32,
            )

    def give(away):
        px = xs[away]
        q[away] = acc[away].astype(BF16).reshape(2, 224, 128)
        for pk in range(2):
            here = (c == px) & (k == pk)

            @pl.when(here)
            def _():
                z_in[c, k] = q[away, pk]

            @pl.when(jnp.logical_not(here))
            def _():
                copy(
                    q.at[away, pk], z_in.at[c, k], z_send.at[away, pk], z_recv.at[c, k],
                    at(x, y, h * 4 + px, pk),
                ).start()

    def run(stage, p, *args):
        if 0 <= p < NP:
            stage(p, *args)

    for m in range(CH // 2):
        form(m)
    acc[...] = jnp.zeros_like(acc)
    arrived(w.at[1 - k], swap_recv.at[1])
    for p in range(NP + LAG_FAR2):
        run(sum_x, p)
        run(sum_y, p - LAG_Y)
        run(spread_other, p - LAG_H)
        run(lambda q: send_own(h, q), p - LAG_OWN)
        run(lambda q: send_near(h, q, False), p - LAG_NEAR)
        run(lambda q: send_own(1 - h, q), p - LAG_OWN2)
        run(lambda q: send_near(1 - h, q, True), p - LAG_NEAR2)
        run(lambda q: multiply(0, h, q), p - LAG_OWN)
        run(lambda q: multiply(0, 1 - h, q), p - LAG_OWN2)
        if p - LAG_OWN2 == NP - 1:
            give(0)
        run(lambda q: multiply(1, h, q), p - LAG_NEAR)
        run(lambda q: multiply(3, h, q), p - LAG_NEAR)
        run(lambda q: multiply(1, 1 - h, q), p - LAG_NEAR2)
        run(lambda q: multiply(3, 1 - h, q), p - LAG_NEAR2)
        if p - LAG_NEAR2 == NP - 1:
            give(1)
            give(3)
        run(lambda q: last(h, q), p - LAG_FAR)
        run(lambda q: multiply(2, h, q), p - LAG_FAR)
        run(lambda q: last(1 - h, q), p - LAG_FAR2)
        run(lambda q: multiply(2, 1 - h, q), p - LAG_FAR2)
    give(2)

    for p in range(NP):
        arrived(gram_in.at[1 - h, pl.ds(*PARTS[p])], h_recv.at[p])
    for ph in range(2):
        for n in range(CH):
            a = 1024 * ph + CW * n
            gram_ref[:, a : a + CW] = gram_in[ph, n]

    sent(wt.at[pl.ds(0, 7)], ring_send)
    sent(g.at[k], swap_send.at[0])
    sent(w.at[k], swap_send.at[1])
    sent(part, x_send)
    sent(y_in, y_send)
    sent(low.at[h], low_send)
    sent(gram_in.at[h], h_send)
    sent(gl.at[0, :, :, pl.ds(0, 7)], ay_send)
    sent(gl.at[pl.ds(0, 2)], ax_send)
    sent(gl.at[0], fw_send)

    for away in range(1, 4):
        for pk in range(2):
            pc = (c + away) % 4
            arrived(z_in.at[pc, pk], z_recv.at[pc, pk])
    arrived(z_in.at[c, 1 - k], z_recv.at[c, 1 - k])
    total = jnp.zeros((224, 256), F32)
    for pk in range(2):
        for pc in range(4):
            total += jnp.dot(z_in[pc, pk], place[pk], preferred_element_type=F32)
    prod_ref[...] = total

    for away in range(4):
        for pk in range(2):

            @pl.when(jnp.logical_not((c == (x + away) % 4) & (k == pk)))
            def _():
                sent(q.at[away, pk], z_send.at[away, pk])


def shards(grad_out, weight):
    dma = pltpu.SemaphoreType.DMA
    return pl.pallas_call(
        kernel,
        name="curvature",
        out_shape=(
            jax.ShapeDtypeStruct((8, 2048), F32),
            jax.ShapeDtypeStruct((224, 256), F32),
        ),
        in_specs=[pl.BlockSpec(memory_space=pltpu.HBM)] * 2,
        out_specs=(pl.BlockSpec(memory_space=pltpu.VMEM),) * 2,
        scratch_shapes=[
            pltpu.VMEM((1024, 128), BF16),
            pltpu.VMEM((2, 1024, 512), BF16),
            pltpu.VMEM((8, 64, 1024), BF16),
            pltpu.VMEM((2, 128, 256), BF16),
            pltpu.VMEM((2, 4, 128, CW), F32),
            pltpu.VMEM((CH, 3, 128, CW), BF16),
            pltpu.VMEM((CH, 128, CW), F32),
            pltpu.VMEM((CH, 3, 128, CW), BF16),
            pltpu.VMEM((CH, 8, 16, CW), F32),
            pltpu.VMEM((CH, 7, 16, CW), F32),
            pltpu.VMEM((CH, 16, CW), F32),
            pltpu.VMEM((2, CH, 8, CW), F32),
            pltpu.VMEM((2, CH, 16, CW), BF16),
            pltpu.VMEM((2, 224, 2048), BF16),
            pltpu.VMEM((4, 2, CH, 8, 16, CW), BF16),
            pltpu.VMEM((4, 448, 128), F32),
            pltpu.VMEM((4, 2, 224, 128), BF16),
            pltpu.VMEM((4, 2, 224, 128), BF16),
            dma((3,)),
            dma((2,)), dma((2,)),
            dma, dma((2, 4, NQ)),
            dma, dma((NP,)),
            dma, dma((NP,)),
            dma, dma((NP,)),
            dma, dma((NP,)),
            dma, dma((2, NP)),
            dma, dma((3, 2, NP)), dma,
            dma((4, 2)), dma((4, 2)),
        ],
        compiler_params=pltpu.CompilerParams(
            collective_id=0, has_side_effects=True, vmem_limit_bytes=53 * 2**20
        ),
        cost_estimate=pl.CostEstimate(flops=2 * 10**9, bytes_accessed=3 * 2**20, transcendentals=0),
    )(grad_out, weight)


def solution(mesh):
    placed = (P("dp", ("col", "row")), P(("dp", "row"), "col"))
    return jax.shard_map(
        shards,
        mesh=mesh,
        in_specs=placed,
        out_specs=(P(("dp", "row"), "col"), P(("dp", "row"), "col")),
        check_vma=False,
    )
```
